512 devices in a mesh: dp: 16 (over y_hi, z), ctx: 32 (over y_lo, x, core).
Axes of the slice: x: 4, y: 8 (y_hi: 2, y_lo: 4; y = y_hi * 4 + y_lo), z: 8, core: 2. Of those that a mesh axis runs over, the one named last changes fastest.
Arguments:
- queries: bfloat16 [16, 4096, 4096], P('dp', 'ctx'), may hold values from -6 to 6
- keys: bfloat16 [16, 4096, 512], P('dp', 'ctx'), may hold values from -6 to 6
- values: bfloat16 [16, 4096, 512], P('dp', 'ctx'), may hold values from -6 to 6
- grad_out: bfloat16 [16, 4096, 4096], P('dp', 'ctx'), may hold values from -6 to 6
- doc_lengths: int32 [16, 8], P('dp'), may hold values from 1 to 2048, 4096 in all within a row
- block_of_slot: int32 [64], replicated, may hold values from 0 to 63, as said below
- partners: int32 [3, 32], replicated, may hold values from 0 to 31, as said below
Outputs:
- attended: bfloat16 [16, 4096, 4096], P('dp', 'ctx')
- grad_queries: bfloat16 [16, 4096, 4096], P('dp', 'ctx')
- grad_keys: bfloat16 [16, 4096, 512], P('dp', 'ctx')
- grad_values: bfloat16 [16, 4096, 512], P('dp', 'ctx')
The draws below stay inside these ranges and needn't reach their ends.
Inputs may be any that keep to these rules, and one draw needn't show every extreme that they name: `block_of_slot`: slots 2k and 2k + 1 are the rows of ctx rank k and hold blocks c and 63 - c; every block appears once. `partners`: in row r every rank i has partner i XOR m_r, where m_r is a power of two, the same for all ranks of the row, and different between rows.
All inputs are finite; a program needn't handle non-finite values.
Results may differ from the reference program's by a relative error of at most 0.034.
Values may be sent and summed in bfloat16 or wider, within the bound.
No kernel may reach another device: no remote copies, remote signals or barrier semaphores. Data moves between devices by JAX's collectives and lax.ppermute only.
A program may use at most 64 MiB of HBM per device.

```python
import math
import jax
import jax.numpy as jnp
import numpy as np
from jax import lax

HQ = 32
KVH = 4
HD = 128
TOK_DEV = 128
ROUNDS = 3
DOCS = 8
HALF = 64
RANKS = 32
SEQS = 16
SEQ_LEN = 4096
MOST_DOC = 2048
CTX_BITS = 5


def planted_rows(key):
    pick_key, sign_key = jax.random.split(key)
    offsets = jax.random.randint(pick_key, (SEQS, RANKS), 1, HALF).astype(jnp.int32)
    signs = jnp.where(jax.random.bernoulli(sign_key, 0.5, (SEQS, RANKS, KVH * HD)), 1.0, -1.0).astype(jnp.float32)
    rows = jnp.arange(SEQ_LEN, dtype=jnp.int32)
    rank_ids = rows // TOK_DEV
    local = rows % TOK_DEV
    offset_rows = offsets[:, rank_ids]
    sign_rows = signs[:, rank_ids, :]
    is_top = (local[None, :] == offset_rows)[:, :, None]
    is_next = (local[None, :] == offset_rows - 1)[:, :, None]
    seq_ids = jnp.arange(SEQS, dtype=jnp.int32)[:, None]
    levels = jnp.array([6.0, 4.5, 3.0], dtype=jnp.float32)
    strength = levels[(rank_ids[None, :] + seq_ids) % 3][:, :, None]
    return (is_top, is_next, sign_rows, strength)


def draw_queries(key, part):
    is_top, is_next, sign_rows, strength = planted_rows(key)
    key = jax.random.fold_in(key, 31)
    shape = (SEQS, SEQ_LEN, HQ * HD)
    base = jnp.clip(jax.random.normal(key, shape, jnp.float32), -6.0, 6.0)
    group_signs = jnp.broadcast_to(sign_rows.reshape(SEQS, SEQ_LEN, KVH, 1, HD), (SEQS, SEQ_LEN, KVH, HQ // KVH, HD)).reshape(shape)
    return jnp.where(is_top, strength * group_signs, base).astype(jnp.bfloat16)


def draw_keys(key, part):
    is_top, is_next, sign_rows, strength = planted_rows(key)
    key = jax.random.fold_in(key, 37)
    shape = (SEQS, SEQ_LEN, KVH * HD)
    base = jnp.clip(jax.random.normal(key, shape, jnp.float32), -6.0, 6.0)
    near = 6.0 - HD ** (-0.5) / 3.0
    planted = jnp.where(is_top, 6.0 * sign_rows, jnp.where(is_next, near * sign_rows, base))
    return planted.astype(jnp.bfloat16)


def draw_block_of_slot(key, part):
    key = jax.random.fold_in(key, 11)
    order = jax.random.permutation(key, RANKS).astype(jnp.int32)
    paired = jnp.stack([order, 2 * RANKS - 1 - order], axis=1)
    return paired.reshape(2 * RANKS).astype(jnp.int32)


def draw_partners(key, part):
    key = jax.random.fold_in(key, 23)
    picks = jax.random.permutation(key, CTX_BITS)[:ROUNDS].astype(jnp.int32)
    masks = jnp.left_shift(jnp.ones_like(picks), picks).astype(jnp.int32)
    rank_ids = jnp.arange(RANKS, dtype=jnp.int32)
    return jnp.bitwise_xor(rank_ids[None, :], masks[:, None]).astype(jnp.int32)


def shard_levels(own_key, dims, shards, least, top_value):
    gain = 1.0
    for axis_at, blocks in shards:
        heights = jax.random.uniform(jax.random.fold_in(jax.random.fold_in(own_key, 6), axis_at), (blocks,), jnp.float32, least / len(shards), top_value / len(shards))
        gain = gain * jnp.repeat(jnp.exp(heights), dims[axis_at] // blocks).reshape((-1,) + (1,) * (len(dims) - 1 - axis_at))
    return gain


def length_profile(amount, total, bound, skew):
    weights = [(1 << 20) // math.isqrt(grade ** skew) + 1 for grade in range(2, amount + 1)]
    surplus, given = total - bound - (amount - 1), [1] * (amount - 1)
    while surplus > 0:
        candidates = [i for i in range(amount - 1) if given[i] < bound]
        mass, remaining = sum([weights[i] for i in candidates]), surplus
        for i in candidates:
            more = min(bound - given[i], max(1, remaining * weights[i] // mass), surplus)
            given[i] = given[i] + more
            surplus = surplus - more
    return np.array([bound] + given)


def uneven_parts(rng, count, total, most, slope):
    if count == 2:
        one = jax.random.randint(rng, (), max(1, total - most), min(most, total - 1) + 1)
        return jnp.stack([one, total - one])
    sizes = jnp.asarray(length_profile(count, total, most, slope), jnp.int32)
    pairs = (count - 1) // 2
    source_of, receiver = sizes[1:1 + 2 * pairs:2], sizes[2:2 + 2 * pairs:2]
    room = jnp.minimum(source_of - 1, most - receiver)
    shifted = jax.random.randint(jax.random.fold_in(rng, 1), (pairs,), 0, 1 << 20) % (room + 1)
    sizes = sizes.at[1:1 + 2 * pairs:2].set(source_of - shifted).at[2:2 + 2 * pairs:2].set(receiver + shifted)
    return sizes[jax.random.permutation(jax.random.fold_in(rng, 2), count)]


def centred(stream_key, extent, deviation, limit, pieces=(), kind=jnp.bfloat16):
    loudness = shard_levels(stream_key, extent, pieces, -0.22, 0.18) if pieces else 1.0
    values = jax.random.normal(stream_key, extent, jnp.float32) * deviation * loudness
    return jnp.minimum(jnp.maximum(values, -limit), limit).astype(kind)


def setup_inputs(seed: int = 0) -> dict:
    streams_of = jax.random.split(jax.random.key(seed), 8)
    queries = draw_queries(jax.random.fold_in(streams_of[7], 71), 0)
    keys = draw_keys(jax.random.fold_in(streams_of[7], 71), 0)
    values = centred(streams_of[2], (SEQS, SEQ_LEN, KVH * HD), 1.0, 6.0, ((0, 16), (1, 32)))
    grad_out = centred(streams_of[3], (SEQS, SEQ_LEN, HQ * HD), 1.0, 6.0, ((0, 16), (1, 32)))
    doc_lengths = jax.vmap(lambda own: uneven_parts(own, DOCS, SEQ_LEN, MOST_DOC, 2))(jax.random.split(streams_of[4], SEQS)).reshape((SEQS, DOCS)).astype(jnp.int32)
    block_of_slot = draw_block_of_slot(jax.random.fold_in(streams_of[7], 71), 0)
    partners = draw_partners(jax.random.fold_in(streams_of[7], 71), 0)
    return dict(queries=queries, keys=keys, values=values, grad_out=grad_out, doc_lengths=doc_lengths, block_of_slot=block_of_slot, partners=partners)


def locate(rank_id, block_of_slot, doc_starts):
    half_rows = TOK_DEV // 2
    index = jnp.arange(TOK_DEV, dtype=jnp.int32)
    slot_id = 2 * rank_id + index // half_rows
    slot_ids = jnp.arange(block_of_slot.shape[0], dtype=jnp.int32)
    block_id = jnp.sum(jnp.where(slot_id[:, None] == slot_ids[None, :], block_of_slot[None, :], 0), axis=1).astype(jnp.int32)
    place = block_id * half_rows + index % half_rows
    doc_ids = jnp.sum((place[:, None] >= doc_starts[None, :]).astype(jnp.int32), axis=1).astype(jnp.int32) - 1
    return place, doc_ids


def attend(query_rows, key_rows, value_rows, grad_rows, allowed):
    tok_rows = query_rows.shape[0]
    group = HQ // KVH
    factor = HD ** -0.5
    outputs, grad_q, grad_k, grad_v = [], [], [], []
    for head_index in range(KVH):
        lower = head_index * group * HD
        upper = lower + group * HD
        query_head = query_rows[:, lower:upper].reshape(tok_rows, group, HD).astype(jnp.float32)
        grad_head = grad_rows[:, lower:upper].reshape(tok_rows, group, HD).astype(jnp.float32)
        key_head = key_rows[:, head_index * HD:(head_index + 1) * HD].astype(jnp.float32)
        value_head = value_rows[:, head_index * HD:(head_index + 1) * HD].astype(jnp.float32)
        scores = jnp.einsum("rgd,kd->grk", query_head, key_head) * factor
        masked = jnp.where(allowed[None], scores, -1e30)
        highest = jnp.max(masked, axis=-1, keepdims=True)
        log_total = highest + jnp.log(jnp.sum(jnp.exp(masked - highest), axis=-1, keepdims=True))
        probs = jnp.exp(masked - log_total)
        probs_b = probs.astype(jnp.bfloat16)
        output = jnp.einsum("grk,kd->rgd", probs_b.astype(jnp.float32), value_head).astype(jnp.bfloat16)
        delta = jnp.sum(grad_head * output.astype(jnp.float32), axis=-1)
        dprob = jnp.einsum("rgd,kd->grk", grad_head, value_head)
        dscore = (probs * (dprob - jnp.transpose(delta)[:, :, None])).astype(jnp.bfloat16)
        dscore_f = dscore.astype(jnp.float32)
        grad_q.append((jnp.einsum("grk,kd->rgd", dscore_f, key_head) * factor).astype(jnp.bfloat16).reshape(tok_rows, group * HD))
        grad_k.append(jnp.einsum("grk,rgd->kd", dscore_f, query_head) * factor)
        grad_v.append(jnp.einsum("grk,rgd->kd", probs_b.astype(jnp.float32), grad_head))
        outputs.append(output.reshape(tok_rows, group * HD))
    return (jnp.concatenate(outputs, axis=1), jnp.concatenate(grad_q, axis=1),
            jnp.concatenate(grad_k, axis=1), jnp.concatenate(grad_v, axis=1))


def reference(queries, keys, values, grad_out, doc_lengths, block_of_slot, partners):
    counts = (SEQ_LEN - doc_lengths[:, DOCS - 1]).astype(jnp.float32)
    weight = jnp.float32(SEQS * SEQ_LEN) / jnp.sum(counts)
    round_masks = partners[:, 0]

    def one_sequence(items):
        seq_q, seq_k, seq_v, seq_g, lengths = items
        doc_ends = jnp.cumsum(lengths).astype(jnp.int32)
        doc_starts = doc_ends - lengths

        def step(carry, rank_id):
            acc_k, acc_v = carry
            mates = jnp.bitwise_xor(rank_id, round_masks).astype(jnp.int32)
            key_ranks = [rank_id] + [mates[index] for index in range(ROUNDS)]
            q_place, q_doc = locate(rank_id, block_of_slot, doc_starts)
            places, docs, key_parts, value_parts = [], [], [], []
            for other in key_ranks:
                place, doc_ids = locate(other, block_of_slot, doc_starts)
                places.append(place)
                docs.append(doc_ids)
                key_parts.append(lax.dynamic_slice_in_dim(seq_k, (other * TOK_DEV).astype(jnp.int32), TOK_DEV, 0))
                value_parts.append(lax.dynamic_slice_in_dim(seq_v, (other * TOK_DEV).astype(jnp.int32), TOK_DEV, 0))
            k_place = jnp.concatenate(places)
            k_doc = jnp.concatenate(docs)
            allowed = (k_place[None, :] <= q_place[:, None]) & (k_doc[None, :] == q_doc[:, None])
            start = (rank_id * TOK_DEV).astype(jnp.int32)
            query_rows = lax.dynamic_slice_in_dim(seq_q, start, TOK_DEV, 0)
            grad_raw = lax.dynamic_slice_in_dim(seq_g, start, TOK_DEV, 0)
            grad_rows = jnp.where((q_doc < DOCS - 1)[:, None], grad_raw.astype(jnp.float32) * weight, 0.0).astype(jnp.bfloat16)
            output, grad_q, grad_k, grad_v = attend(query_rows, jnp.concatenate(key_parts), jnp.concatenate(value_parts), grad_rows, allowed)
            for index, other in enumerate(key_ranks):
                where_at = (other * TOK_DEV).astype(jnp.int32)
                piece_k = lax.dynamic_slice_in_dim(acc_k, where_at, TOK_DEV, 0) + grad_k[index * TOK_DEV:(index + 1) * TOK_DEV]
                acc_k = lax.dynamic_update_slice_in_dim(acc_k, piece_k, where_at, 0)
                piece_v = lax.dynamic_slice_in_dim(acc_v, where_at, TOK_DEV, 0) + grad_v[index * TOK_DEV:(index + 1) * TOK_DEV]
                acc_v = lax.dynamic_update_slice_in_dim(acc_v, piece_v, where_at, 0)
            return (acc_k, acc_v), (output, grad_q)

        zeros_kv = jnp.zeros((SEQ_LEN, KVH * HD), jnp.float32)
        (acc_k, acc_v), (outputs, grads) = lax.scan(step, (zeros_kv, zeros_kv), jnp.arange(RANKS, dtype=jnp.int32))
        return (outputs.reshape(SEQ_LEN, HQ * HD), grads.reshape(SEQ_LEN, HQ * HD),
                acc_k.astype(jnp.bfloat16), acc_v.astype(jnp.bfloat16))

    attended, grad_queries, grad_keys, grad_values = lax.map(one_sequence, (queries, keys, values, grad_out, doc_lengths))
    return (attended, grad_queries, grad_keys, grad_values)
```

```python
import functools
import itertools

import jax
import jax.numpy as jnp
from jax import lax
from jax.experimental import pallas as pl
from jax.experimental.pallas import tpu as pltpu
from jax.sharding import PartitionSpec as P

HQ = 32
KVH = 4
HD = 128
GROUP = HQ // KVH
FACTOR = HD ** (-0.5)
LOG2E = 1.4426950408889634
BF16 = jnp.bfloat16
F32 = jnp.float32


def swapped(value, axis, mask):
    pairs = [(source, source ^ mask) for source in range(lax.axis_size(axis))]
    return lax.ppermute(value, axis, pairs)


def places(slots_ref, rank, half, shape, dim):
    at = lax.broadcasted_iota(jnp.int32, shape, dim)
    low = slots_ref[2 * rank] * half
    high = slots_ref[2 * rank + 1] * half - half
    return at + jnp.where(at < half, low, high)


def documents(place, lengths_ref):
    start = jnp.int32(0)
    doc = jnp.zeros_like(place)
    for index in range(lengths_ref.shape[1] - 1):
        start = start + lengths_ref[0, index]
        doc = doc + (place >= start).astype(jnp.int32)
    return doc


def dot(a, b):
    return jnp.dot(a, b, preferred_element_type=F32)


def dot_nt(a, b):
    return lax.dot_general(a, b, (((1,), (1,)), ((), ())), preferred_element_type=F32)


def attention_kernel(masks, rank_ref, lengths_ref, slots_ref, q_ref, g_ref, k_ref, v_ref, *rest):
    count = len(masks)
    received = rest[:count]
    out_ref, gq_ref, own_ref = rest[count : count + 3]
    back = rest[count + 3 : 2 * count + 3]
    bias_ref, valid_ref, kk, vv, kt_ref, vt_ref = rest[2 * count + 3 :]
    tok = q_ref.shape[0]
    docs = lengths_ref.shape[1]

    @pl.when(pl.program_id(0) == 0)
    def _():
        rank = rank_ref[0]
        half = tok // 2
        q_place = places(slots_ref, rank, half, (1, tok), 1)
        q_doc = documents(q_place, lengths_ref)
        valid_ref[...] = (q_doc < docs - 1).astype(F32)
        for index, mask in enumerate((0,) + masks):
            k_place = places(slots_ref, rank ^ mask, half, (tok, 1), 0)
            k_doc = documents(k_place, lengths_ref)
            allowed = (k_place <= q_place) & (k_doc == q_doc)
            bias_ref[index * tok : (index + 1) * tok, :] = jnp.where(allowed, 0.0, -1e30)

    kk[0:tok] = k_ref[...]
    vv[0:tok] = v_ref[...]
    for index in range(count):
        kk[(index + 1) * tok : (index + 2) * tok] = received[index][0]
        vv[(index + 1) * tok : (index + 2) * tok] = received[index][1]
    kt_ref[...] = kk[...].T
    vt_ref[...] = vv[...].T
    bias = jnp.concatenate([bias_ref[...]] * GROUP, axis=1)
    valid = jnp.concatenate([valid_ref[...]] * GROUP, axis=1)

    def head(ref, index):
        return ref[:, index * HD : (index + 1) * HD]

    q = jnp.concatenate([head(q_ref, index) for index in range(GROUP)], axis=0)
    g_t = jnp.concatenate([head(g_ref, index).T for index in range(GROUP)], axis=1)
    scores = dot_nt(kk[...], q) * (FACTOR * LOG2E) + bias
    highest = jnp.max(scores, axis=0, keepdims=True)
    probs = jnp.exp2(scores - highest)
    inverse = 1.0 / jnp.sum(probs, axis=0, keepdims=True)
    probs_b = probs.astype(BF16)
    out_t = (dot(vt_ref[...], probs_b) * inverse).astype(BF16)
    g_t = (g_t.astype(F32) * (inverse * valid)).astype(BF16)
    delta = jnp.sum(g_t.astype(F32) * out_t.astype(F32), axis=0, keepdims=True)
    dscore = (probs * (dot(vv[...], g_t) - delta)).astype(BF16)
    gq_t = (dot(kt_ref[...], dscore) * FACTOR).astype(BF16)
    for index in range(GROUP):
        out_ref[:, index * HD : (index + 1) * HD] = head(out_t, index).T
        gq_ref[:, index * HD : (index + 1) * HD] = head(gq_t, index).T
    grad_k = dot(dscore, q) * FACTOR
    grad_v = dot_nt(probs_b, g_t)
    own_ref[0] = grad_k[0:tok]
    own_ref[1] = grad_v[0:tok]
    for index in range(count):
        back[index][0] = grad_k[(index + 1) * tok : (index + 2) * tok].astype(BF16)
        back[index][1] = grad_v[(index + 1) * tok : (index + 2) * tok].astype(BF16)


def attention(masks, rank, lengths, slots, queries, grad_out, keys, values, received):
    count = len(masks)
    tok = queries.shape[1]
    kv_heads = keys.shape[2] // HD
    wide = GROUP * HD
    rows = (count + 1) * tok
    smem = pl.BlockSpec(memory_space=pltpu.SMEM)
    row = pl.BlockSpec((None, tok, wide), lambda j: (0, 0, j))
    own = pl.BlockSpec((None, tok, HD), lambda j: (0, 0, j))
    pair = pl.BlockSpec((2, tok, HD), lambda j: (0, 0, j))
    flops = 6 * 2 * rows * tok * HD * GROUP * kv_heads
    moved = 4 * queries.size * 2 + (2 * count + 1) * received[0].size * 2
    return pl.pallas_call(
        functools.partial(attention_kernel, masks),
        grid=(kv_heads,),
        in_specs=[smem, smem, smem, row, row, own, own] + [pair] * count,
        out_specs=[row, row, pair] + [pair] * count,
        out_shape=[
            jax.ShapeDtypeStruct(queries.shape, BF16),
            jax.ShapeDtypeStruct(queries.shape, BF16),
            jax.ShapeDtypeStruct((2, tok, kv_heads * HD), F32),
        ]
        + [jax.ShapeDtypeStruct((2, tok, kv_heads * HD), BF16)] * count,
        scratch_shapes=[
            pltpu.VMEM((rows, tok), F32),
            pltpu.VMEM((1, tok), F32),
            pltpu.VMEM((rows, HD), BF16),
            pltpu.VMEM((rows, HD), BF16),
            pltpu.VMEM((HD, rows), BF16),
            pltpu.VMEM((HD, rows), BF16),
        ],
        compiler_params=pltpu.CompilerParams(vmem_limit_bytes=48 * 2**20),
        cost_estimate=pl.CostEstimate(
            flops=flops, bytes_accessed=moved, transcendentals=rows * tok * GROUP * kv_heads
        ),
        name="attention",
    )(rank, lengths, slots, queries, grad_out, keys, values, *received)


def prepare_kernel(codes, partners_ref, k_ref, v_ref, both_ref, which_ref):
    used = partners_ref[0, 0]
    for index in range(1, partners_ref.shape[0]):
        used = used | partners_ref[index, 0]
    which = jnp.int32(0)
    for index, code in enumerate(codes):
        which = jnp.where(used == code, index, which)
    which_ref[0] = which
    both_ref[0] = k_ref[0]
    both_ref[1] = v_ref[0]


def prepare(codes, partners, keys, values):
    vmem = pl.BlockSpec(memory_space=pltpu.VMEM)
    smem = pl.BlockSpec(memory_space=pltpu.SMEM)
    return pl.pallas_call(
        functools.partial(prepare_kernel, codes),
        in_specs=[smem, vmem, vmem],
        out_specs=[vmem, smem],
        out_shape=[
            jax.ShapeDtypeStruct((2,) + keys.shape[1:], BF16),
            jax.ShapeDtypeStruct((1,), jnp.int32),
        ],
        name="prepare",
    )(partners, keys, values)


def added(padding, step):
    return padding + swapped(padding, "dp", 1 << step)


def with_partners(bits, queries, keys, values, grad_out, lengths, slots, both):
    masks = tuple(1 << bit for bit in bits)
    tok = queries.shape[1]
    rank = lax.axis_index("ctx").astype(jnp.int32).reshape(1)
    received = [swapped(both, "ctx", mask) for mask in masks]
    seqs = lax.axis_size("dp")
    steps = sorted(range(seqs.bit_length() - 1), key=lambda step: (step + 2) % 4)
    padding = lengths
    for step in steps[:2]:
        padding = added(padding, step)
    outs = attention(masks, rank, lengths, slots, queries, grad_out, keys, values, received)
    attended, grad_q, total = outs[:3]
    back = outs[3:]
    padding, back = lax.optimization_barrier((padding, back))
    returned = [swapped(part, "ctx", mask) for part, mask in zip(back, masks)]
    for step in steps[2:]:
        padding = added(padding, step)
    all_tokens = seqs * tok * lax.axis_size("ctx")
    padded = padding[0, lengths.shape[1] - 1]
    weight = F32(all_tokens) / (all_tokens - padded).astype(F32)
    for part in returned:
        total = total + part.astype(F32)
    total = (total * weight).astype(BF16)
    grad_q = (grad_q.astype(F32) * weight).astype(BF16)
    return attended, grad_q, total[0][None], total[1][None]


def on_device(queries, keys, values, grad_out, doc_lengths, block_of_slot, partners):
    rounds = partners.shape[0]
    bit_count = lax.axis_size("ctx").bit_length() - 1
    choices = list(itertools.combinations(range(bit_count), rounds))
    codes = [sum(1 << bit for bit in bits) for bits in choices]
    both, which = prepare(codes, partners, keys, values)
    branches = [functools.partial(with_partners, bits) for bits in choices]
    return lax.switch(
        which[0], branches, queries, keys, values, grad_out, doc_lengths, block_of_slot, both
    )


def solution(mesh):
    rows = P("dp", "ctx", None)
    in_specs = (rows, rows, rows, rows, P("dp", None), P(), P())
    return jax.shard_map(
        on_device, mesh=mesh, in_specs=in_specs, out_specs=(rows,) * 4, check_vma=False
    )
```

```python
import functools
import itertools

import jax
import jax.numpy as jnp
from jax import lax
from jax.experimental import pallas as pl
from jax.experimental.pallas import tpu as pltpu
from jax.sharding import PartitionSpec as P

HQ = 32
KVH = 4
HD = 128
GROUP = HQ // KVH
FACTOR = HD ** (-0.5)
LOG2E = 1.4426950408889634
BF16 = jnp.bfloat16
F32 = jnp.float32


def swapped(value, axis, mask):
    pairs = [(source, source ^ mask) for source in range(lax.axis_size(axis))]
    return lax.ppermute(value, axis, pairs)


def documents(place, lengths_ref):
    start = jnp.int32(0)
    doc = jnp.zeros_like(place)
    for index in range(lengths_ref.shape[1] - 1):
        start = start + lengths_ref[0, index]
        doc = doc + (place >= start).astype(jnp.int32)
    return doc


def dot(a, b):
    return jnp.dot(a, b, preferred_element_type=F32)


def dot_nt(a, b):
    return lax.dot_general(a, b, (((1,), (1,)), ((), ())), preferred_element_type=F32)


def block_places(slots_ref, rank, half):
    first, second = slots_ref[2 * rank], slots_ref[2 * rank + 1]
    low_row = pl.multiple_of(jnp.where(first < second, 0, half), half)
    high_row = pl.multiple_of(half - low_row, half)
    low, high = jnp.minimum(first, second), jnp.maximum(first, second)
    return (low * half, high * half), (pl.ds(low_row, half), pl.ds(high_row, half))


def mask_scores(theirs, lengths_ref, bias_refs, valid_refs):
    docs = lengths_ref.shape[1]
    lanes = valid_refs[0].shape[1]
    half = theirs[0][1][0].size
    lane = lax.broadcasted_iota(jnp.int32, (1, lanes), 1) % half
    row = lax.broadcasted_iota(jnp.int32, (half, 1), 0)
    for side in range(2):
        q_place = lane + theirs[0][0][side]
        q_doc = documents(q_place, lengths_ref)
        valid_refs[side][...] = (q_doc < docs - 1).astype(F32)
        for level in range(side + 1):
            for index, (starts, _) in enumerate(theirs):
                k_place = row + starts[level]
                k_doc = documents(k_place, lengths_ref)
                allowed = (k_place <= q_place) & (k_doc == q_doc)
                at = (level * len(theirs) + index) * half
                bias_refs[side][at : at + half, :] = jnp.where(allowed, 0.0, -1e30)


def attention_kernel(count, *refs):
    rank_ref, which_ref, lengths_ref, slots_ref, q_ref, g_ref, k_ref, v_ref = refs[:8]
    rest = refs[8:]
    received = rest[:count]
    out_ref, gq_ref, own_ref = rest[count : count + 3]
    back = rest[count + 3 : 2 * count + 3]
    bias_refs, valid_refs = rest[2 * count + 3 : 2 * count + 5], rest[2 * count + 5 : 2 * count + 7]
    kk, vv, kt_ref, vt_ref = rest[2 * count + 7 :]
    half = q_ref.shape[0] // 2
    heads = kk.shape[0]
    lows = (count + 1) * half
    rank = rank_ref[0]
    ranks = [rank] + [rank ^ which_ref[index + 1] for index in range(count)]
    theirs = [block_places(slots_ref, other, half) for other in ranks]

    @pl.when(pl.program_id(0) == 0)
    def _():
        mask_scores(theirs, lengths_ref, bias_refs, valid_refs)

    for head in range(heads):
        cols = slice(head * HD, (head + 1) * HD)
        for level in range(2):
            for index, (_, rows) in enumerate(theirs):
                at = level * lows + index * half
                rows = rows[level]
                if index == 0:
                    kk[head, at : at + half] = k_ref[rows, cols]
                    vv[head, at : at + half] = v_ref[rows, cols]
                else:
                    kk[head, at : at + half] = received[index - 1][0, rows, cols]
                    vv[head, at : at + half] = received[index - 1][1, rows, cols]
        kt_ref[head] = kk[head].T
        vt_ref[head] = vv[head].T
    repeats = GROUP * half // valid_refs[0].shape[1]
    partial = {}

    def steps(head, side):
        size = (side + 1) * lows
        rows = theirs[0][1][side]
        key, value = kk[head, 0:size], vv[head, 0:size]
        columns = [slice(at * HD, (at + 1) * HD) for at in range(head * GROUP, (head + 1) * GROUP)]
        q = jnp.concatenate([q_ref[rows, cols] for cols in columns], axis=0)
        g_t = jnp.concatenate([g_ref[rows, cols] for cols in columns], axis=0).T
        scores = dot_nt(key, q)
        yield
        bias = jnp.concatenate([bias_refs[side][...]] * repeats, axis=1)
        valid = jnp.concatenate([valid_refs[side][...]] * repeats, axis=1)
        scores = scores * (FACTOR * LOG2E) + bias
        probs = jnp.exp2(scores - jnp.max(scores, axis=0, keepdims=True))
        inverse = 1.0 / jnp.sum(probs, axis=0, keepdims=True)
        probs_b = probs.astype(BF16)
        g_t = (g_t.astype(F32) * (inverse * valid)).astype(BF16)
        yield
        out_t = dot(vt_ref[head, :, 0:size], probs_b)
        dprob = dot(value, g_t)
        grad_v = dot_nt(probs_b, g_t)
        yield
        out_t = (out_t * inverse).astype(BF16)
        delta = jnp.sum(g_t.astype(F32) * out_t.astype(F32), axis=0, keepdims=True)
        dscore = (probs * (dprob - delta)).astype(BF16)
        yield
        gq_t = dot(kt_ref[head, :, 0:size], dscore)
        grad_k = dot(dscore, q)
        yield
        out = out_t.T
        gq = (gq_t * FACTOR).astype(BF16).T
        for index, cols in enumerate(columns):
            out_ref[rows, cols] = out[index * half : (index + 1) * half]
            gq_ref[rows, cols] = gq[index * half : (index + 1) * half]
        partial[head, side] = (grad_k * FACTOR, grad_v)

    waiting = [steps(head, side) for head in range(heads) for side in (1, 0)]
    running = []
    while waiting or running:
        if waiting:
            running.append(waiting.pop(0))
        running = [chain for chain in running if next(chain, running) is not running]

    for head in range(heads):
        cols = slice(head * HD, (head + 1) * HD)
        for which in range(2):
            high, low = partial[head, 1][which], partial[head, 0][which]
            for level in range(2):
                for index, (_, rows) in enumerate(theirs):
                    at = level * lows + index * half
                    piece = high[at : at + half]
                    if level == 0:
                        piece = piece + low[at : at + half]
                    if index == 0:
                        own_ref[which, rows[level], cols] = piece
                    else:
                        back[index - 1][which, rows[level], cols] = piece.astype(BF16)


def attention(rank, which, lengths, slots, queries, grad_out, keys, values, received):
    count = len(received)
    tok = queries.shape[1]
    kv_heads = keys.shape[2] // HD
    heads = 2
    wide = GROUP * HD * heads
    rows = (count + 1) * tok
    smem = pl.BlockSpec(memory_space=pltpu.SMEM)
    row = pl.BlockSpec((None, tok, wide), lambda j: (0, 0, j))
    own = pl.BlockSpec((None, tok, HD * heads), lambda j: (0, 0, j))
    pair = pl.BlockSpec((2, tok, HD * heads), lambda j: (0, 0, j))
    flops = 6 * 2 * rows * tok * HD * GROUP * kv_heads
    moved = 4 * queries.size * 2 + (2 * count + 1) * received[0].size * 2
    return pl.pallas_call(
        functools.partial(attention_kernel, count),
        grid=(kv_heads // heads,),
        in_specs=[smem] * 4 + [row, row, own, own] + [pair] * count,
        out_specs=[row, row, pair] + [pair] * count,
        out_shape=[
            jax.ShapeDtypeStruct(queries.shape, BF16),
            jax.ShapeDtypeStruct(queries.shape, BF16),
            jax.ShapeDtypeStruct((2, tok, kv_heads * HD), F32),
        ]
        + [jax.ShapeDtypeStruct((2, tok, kv_heads * HD), BF16)] * count,
        scratch_shapes=[
            pltpu.VMEM((rows // 2, tok), F32),
            pltpu.VMEM((rows, tok), F32),
            pltpu.VMEM((1, tok), F32),
            pltpu.VMEM((1, tok), F32),
            pltpu.VMEM((heads, rows, HD), BF16),
            pltpu.VMEM((heads, rows, HD), BF16),
            pltpu.VMEM((heads, HD, rows), BF16),
            pltpu.VMEM((heads, HD, rows), BF16),
        ],
        compiler_params=pltpu.CompilerParams(vmem_limit_bytes=60 * 2**20),
        cost_estimate=pl.CostEstimate(
            flops=flops, bytes_accessed=moved, transcendentals=rows * tok * GROUP * kv_heads
        ),
        name="attention",
    )(rank, which, lengths, slots, queries, grad_out, keys, values, *received)


def prepare_kernel(choices, partners_ref, k_ref, v_ref, both_ref, which_ref):
    used = partners_ref[0, 0]
    for index in range(1, partners_ref.shape[0]):
        used = used | partners_ref[index, 0]
    found = [jnp.int32(0)] * which_ref.shape[0]
    for index, bits in enumerate(choices):
        hit = used == sum(1 << bit for bit in bits)
        wanted = [index] + [1 << bit for bit in bits]
        found = [jnp.where(hit, new, old) for new, old in zip(wanted, found)]
    for index, value in enumerate(found):
        which_ref[index] = value
    both_ref[0] = k_ref[0]
    both_ref[1] = v_ref[0]


def prepare(choices, partners, keys, values):
    vmem = pl.BlockSpec(memory_space=pltpu.VMEM)
    smem = pl.BlockSpec(memory_space=pltpu.SMEM)
    return pl.pallas_call(
        functools.partial(prepare_kernel, choices),
        in_specs=[smem, vmem, vmem],
        out_specs=[vmem, smem],
        out_shape=[
            jax.ShapeDtypeStruct((2,) + keys.shape[1:], BF16),
            jax.ShapeDtypeStruct((1 + partners.shape[0],), jnp.int32),
        ],
        compiler_params=pltpu.CompilerParams(vmem_limit_bytes=60 * 2**20),
        name="prepare",
    )(partners, keys, values)


def loss_weight(all_tokens, padding_refs, width):
    last = padding_refs[0].shape[1] - 1
    padded = padding_refs[0][0, last] + padding_refs[1][0, last]
    return F32(all_tokens) / jnp.full((1, width), all_tokens - padded, jnp.int32).astype(F32)


def finish_kernel(all_tokens, count, half_ref, other_ref, gq_ref, own_ref, *rest):
    parts, outs, scratch = rest[:count], rest[count : count + 3], rest[count + 3 :]
    scaled, summed, sems = scratch
    width = scaled.shape[2]
    weight = loss_weight(all_tokens, (half_ref, other_ref), width)
    copies = []

    def send(source, target):
        copy = pltpu.make_async_copy(source, target, sems.at[len(copies)])
        copy.start()
        copies.append(copy)

    for part in range(scaled.shape[0]):
        cols = slice(part * width, (part + 1) * width)
        scaled[part] = (gq_ref[0, :, cols].astype(F32) * weight).astype(BF16)
        send(scaled.at[part], outs[0].at[0, :, cols])
    for which in range(2):
        value = own_ref[which]
        for part in parts:
            value = value + part[which].astype(F32)
        summed[which] = (value * weight[:, : value.shape[1]]).astype(BF16)
        send(summed.at[which], outs[which + 1].at[0])
    for copy in copies:
        copy.wait()


def finish(all_tokens, half, other, grad_q, own, parts):
    smem = pl.BlockSpec(memory_space=pltpu.SMEM)
    vmem = pl.BlockSpec(memory_space=pltpu.VMEM)
    hbm = pl.BlockSpec(memory_space=pltpu.HBM)
    pieces = 4
    keys = jax.ShapeDtypeStruct((1,) + own.shape[1:], BF16)
    return pl.pallas_call(
        functools.partial(finish_kernel, all_tokens, len(parts)),
        in_specs=[smem, smem] + [vmem] * (2 + len(parts)),
        out_specs=[hbm] * 3,
        out_shape=[jax.ShapeDtypeStruct(grad_q.shape, BF16), keys, keys],
        scratch_shapes=[
            pltpu.VMEM((pieces, grad_q.shape[1], grad_q.shape[2] // pieces), BF16),
            pltpu.VMEM(own.shape, BF16),
            pltpu.SemaphoreType.DMA((pieces + 2,)),
        ],
        compiler_params=pltpu.CompilerParams(vmem_limit_bytes=60 * 2**20),
        name="finish",
    )(half, other, grad_q, own, *parts)


def fetch(bits, step, both, lengths):
    received = [swapped(both, "ctx", 1 << bit) for bit in bits]
    return received, lengths + swapped(lengths, "dp", step)


def give_back(bits, steps, back, padding):
    far, *near = reversed(list(zip(bits, back)))
    returned = [swapped(far[1], "ctx", 1 << far[0])]
    other = swapped(padding, "dp", steps[0])
    returned += [swapped(part, "ctx", 1 << bit) for bit, part in near]
    padding = padding + other
    return returned, padding, swapped(padding, "dp", steps[1])


def on_device(queries, keys, values, grad_out, doc_lengths, block_of_slot, partners):
    rounds = partners.shape[0]
    seqs, ranks = lax.axis_size("dp"), lax.axis_size("ctx")
    choices = list(itertools.combinations(range(ranks.bit_length() - 1), rounds))
    steps = [1 << step for step in reversed(range(seqs.bit_length() - 1))]
    rank = lax.axis_index("ctx").astype(jnp.int32).reshape(1)
    both, which = prepare(choices, partners, keys, values)
    fetches = [functools.partial(fetch, bits, steps[0]) for bits in choices]
    received, padding = lax.switch(which[0], fetches, both, doc_lengths)
    other = swapped(padding, "dp", steps[1])
    attended, grad_q, own, *back = attention(
        rank, which, doc_lengths, block_of_slot, queries, grad_out, keys, values, received
    )
    other, back = lax.optimization_barrier((other, back))
    gives = [functools.partial(give_back, bits, steps[2:]) for bits in choices]
    returned, padding, other = lax.switch(which[0], gives, back, padding + other)
    all_tokens = seqs * ranks * queries.shape[1]
    grad_q, grad_k, grad_v = finish(all_tokens, padding, other, grad_q, own, returned)
    return attended, grad_q, grad_k, grad_v


def solution(mesh):
    rows = P("dp", "ctx", None)
    in_specs = (rows, rows, rows, rows, P("dp", None), P(), P())
    return jax.shard_map(
        on_device, mesh=mesh, in_specs=in_specs, out_specs=(rows,) * 4, check_vma=False
    )
```

```python
import functools
import itertools

import jax
import jax.numpy as jnp
from jax import lax
from jax.experimental import pallas as pl
from jax.experimental.pallas import tpu as pltpu
from jax.sharding import PartitionSpec as P

HQ = 32
KVH = 4
HD = 128
GROUP = HQ // KVH
FACTOR = HD ** (-0.5)
LOG2E = 1.4426950408889634
BF16 = jnp.bfloat16
F32 = jnp.float32


def swapped(value, axis, mask):
    pairs = [(source, source ^ mask) for source in range(lax.axis_size(axis))]
    return lax.ppermute(value, axis, pairs)


def documents(place, lengths_ref):
    start = jnp.int32(0)
    doc = jnp.zeros_like(place)
    for index in range(lengths_ref.shape[1] - 1):
        start = start + lengths_ref[0, index]
        doc = doc + (place >= start).astype(jnp.int32)
    return doc


def dot(a, b):
    return jnp.dot(a, b, preferred_element_type=F32)


def dot_nt(a, b):
    return lax.dot_general(a, b, (((1,), (1,)), ((), ())), preferred_element_type=F32)


def block_places(slots_ref, rank, half):
    first, second = slots_ref[2 * rank], slots_ref[2 * rank + 1]
    low_row = pl.multiple_of(jnp.where(first < second, 0, half), half)
    high_row = pl.multiple_of(half - low_row, half)
    low, high = jnp.minimum(first, second), jnp.maximum(first, second)
    return (low * half, high * half), (pl.ds(low_row, half), pl.ds(high_row, half))


def mask_scores(theirs, lengths_ref, bias_refs, valid_refs):
    docs = lengths_ref.shape[1]
    lanes = valid_refs[0].shape[1]
    half = theirs[0][1][0].size
    lane = lax.broadcasted_iota(jnp.int32, (1, lanes), 1) % half
    row = lax.broadcasted_iota(jnp.int32, (half, 1), 0)
    for side in range(2):
        q_place = lane + theirs[0][0][side]
        q_doc = documents(q_place, lengths_ref)
        valid_refs[side][...] = (q_doc < docs - 1).astype(F32)
        for level in range(side + 1):
            for index, (starts, _) in enumerate(theirs):
                k_place = row + starts[level]
                k_doc = documents(k_place, lengths_ref)
                allowed = (k_place <= q_place) & (k_doc == q_doc)
                at = (level * len(theirs) + index) * half
                bias_refs[side][at : at + half, :] = jnp.where(allowed, 0.0, -1e30)


def attention_kernel(count, *refs):
    rank_ref, which_ref, lengths_ref, slots_ref, q_ref, g_ref, k_ref, v_ref = refs[:8]
    rest = refs[8:]
    received = rest[:count]
    out_ref, gq_ref, own_ref = rest[count : count + 3]
    back = rest[count + 3 : 2 * count + 3]
    bias_refs, valid_refs = rest[2 * count + 3 : 2 * count + 5], rest[2 * count + 5 : 2 * count + 7]
    kk, vv, kt_ref, vt_ref = rest[2 * count + 7 :]
    half = q_ref.shape[0] // 2
    heads = kk.shape[0]
    lows = (count + 1) * half
    rank = rank_ref[0]
    ranks = [rank] + [rank ^ which_ref[index + 1] for index in range(count)]
    theirs = [block_places(slots_ref, other, half) for other in ranks]

    @pl.when(pl.program_id(0) == 0)
    def _():
        mask_scores(theirs, lengths_ref, bias_refs, valid_refs)

    for head in range(heads):
        cols = slice(head * HD, (head + 1) * HD)
        for level in range(2):
            for index, (_, rows) in enumerate(theirs):
                at = level * lows + index * half
                rows = rows[level]
                if index == 0:
                    kk[head, at : at + half] = k_ref[rows, cols]
                    vv[head, at : at + half] = v_ref[rows, cols]
                else:
                    kk[head, at : at + half] = received[index - 1][0, rows, cols]
                    vv[head, at : at + half] = received[index - 1][1, rows, cols]
        kt_ref[head] = kk[head].T
        vt_ref[head] = vv[head].T
    repeats = GROUP * half // valid_refs[0].shape[1]
    partial = {}

    def steps(head, side):
        size = (side + 1) * lows
        rows = theirs[0][1][side]
        key, value = kk[head, 0:size], vv[head, 0:size]
        columns = [slice(at * HD, (at + 1) * HD) for at in range(head * GROUP, (head + 1) * GROUP)]
        q = jnp.concatenate([q_ref[rows, cols] for cols in columns], axis=0)
        g_t = jnp.concatenate([g_ref[rows, cols] for cols in columns], axis=0).T
        scores = dot_nt(key, q)
        yield
        bias = jnp.concatenate([bias_refs[side][...]] * repeats, axis=1)
        valid = jnp.concatenate([valid_refs[side][...]] * repeats, axis=1)
        scores = scores * (FACTOR * LOG2E) + bias
        probs = jnp.exp2(scores - jnp.max(scores, axis=0, keepdims=True))
        inverse = 1.0 / jnp.sum(probs, axis=0, keepdims=True)
        probs_b = probs.astype(BF16)
        g_t = (g_t.astype(F32) * (inverse * valid)).astype(BF16)
        yield
        out_t = dot(vt_ref[head, :, 0:size], probs_b)
        dprob = dot(value, g_t)
        grad_v = dot_nt(probs_b, g_t)
        yield
        out_t = (out_t * inverse).astype(BF16)
        delta = jnp.sum(g_t.astype(F32) * out_t.astype(F32), axis=0, keepdims=True)
        dscore = (probs * (dprob - delta)).astype(BF16)
        yield
        gq_t = dot(kt_ref[head, :, 0:size], dscore)
        grad_k = dot(dscore, q)
        yield
        out = out_t.T
        gq = (gq_t * FACTOR).astype(BF16).T
        for index, cols in enumerate(columns):
            out_ref[rows, cols] = out[index * half : (index + 1) * half]
            gq_ref[rows, cols] = gq[index * half : (index + 1) * half]
        partial[head, side] = (grad_k * FACTOR, grad_v)

    waiting = [steps(head, side) for head in range(heads) for side in (1, 0)]
    running = []
    while waiting or running:
        if waiting:
            running.append(waiting.pop(0))
        running = [chain for chain in running if next(chain, running) is not running]

    for head in range(heads):
        cols = slice(head * HD, (head + 1) * HD)
        for which in range(2):
            high, low = partial[head, 1][which], partial[head, 0][which]
            for level in range(2):
                for index, (_, rows) in enumerate(theirs):
                    at = level * lows + index * half
                    piece = high[at : at + half]
                    if level == 0:
                        piece = piece + low[at : at + half]
                    if index == 0:
                        own_ref[which, rows[level], cols] = piece
                    else:
                        back[index - 1][which, rows[level], cols] = piece.astype(BF16)


def attention(rank, which, lengths, slots, queries, grad_out, keys, values, received):
    count = len(received)
    tok = queries.shape[1]
    kv_heads = keys.shape[2] // HD
    heads = 2
    wide = GROUP * HD * heads
    rows = (count + 1) * tok
    smem = pl.BlockSpec(memory_space=pltpu.SMEM)
    row = pl.BlockSpec((None, tok, wide), lambda j: (0, 0, j))
    own = pl.BlockSpec((None, tok, HD * heads), lambda j: (0, 0, j))
    pair = pl.BlockSpec((2, tok, HD * heads), lambda j: (0, 0, j))
    flops = 6 * 2 * rows * tok * HD * GROUP * kv_heads
    moved = 4 * queries.size * 2 + (2 * count + 1) * received[0].size * 2
    return pl.pallas_call(
        functools.partial(attention_kernel, count),
        grid=(kv_heads // heads,),
        in_specs=[smem] * 4 + [row, row, own, own] + [pair] * count,
        out_specs=[row, row, pair] + [pair] * count,
        out_shape=[
            jax.ShapeDtypeStruct(queries.shape, BF16),
            jax.ShapeDtypeStruct(queries.shape, BF16),
            jax.ShapeDtypeStruct((2, tok, kv_heads * HD), F32),
        ]
        + [jax.ShapeDtypeStruct((2, tok, kv_heads * HD), BF16)] * count,
        scratch_shapes=[
            pltpu.VMEM((rows // 2, tok), F32),
            pltpu.VMEM((rows, tok), F32),
            pltpu.VMEM((1, tok), F32),
            pltpu.VMEM((1, tok), F32),
            pltpu.VMEM((heads, rows, HD), BF16),
            pltpu.VMEM((heads, rows, HD), BF16),
            pltpu.VMEM((heads, HD, rows), BF16),
            pltpu.VMEM((heads, HD, rows), BF16),
        ],
        compiler_params=pltpu.CompilerParams(vmem_limit_bytes=60 * 2**20),
        cost_estimate=pl.CostEstimate(
            flops=flops, bytes_accessed=moved, transcendentals=rows * tok * GROUP * kv_heads
        ),
        name="attention",
    )(rank, which, lengths, slots, queries, grad_out, keys, values, *received)


def prepare_kernel(choices, partners_ref, k_ref, v_ref, both_ref, which_ref):
    used = partners_ref[0, 0]
    for index in range(1, partners_ref.shape[0]):
        used = used | partners_ref[index, 0]
    found = [jnp.int32(0)] * which_ref.shape[0]
    for index, bits in enumerate(choices):
        hit = used == sum(1 << bit for bit in bits)
        wanted = [index] + [1 << bit for bit in bits]
        found = [jnp.where(hit, new, old) for new, old in zip(wanted, found)]
    for index, value in enumerate(found):
        which_ref[index] = value
    both_ref[0] = k_ref[0]
    both_ref[1] = v_ref[0]


def prepare(choices, partners, keys, values):
    vmem = pl.BlockSpec(memory_space=pltpu.VMEM)
    smem = pl.BlockSpec(memory_space=pltpu.SMEM)
    return pl.pallas_call(
        functools.partial(prepare_kernel, choices),
        in_specs=[smem, vmem, vmem],
        out_specs=[vmem, smem],
        out_shape=[
            jax.ShapeDtypeStruct((2,) + keys.shape[1:], BF16),
            jax.ShapeDtypeStruct((1 + partners.shape[0],), jnp.int32),
        ],
        compiler_params=pltpu.CompilerParams(vmem_limit_bytes=60 * 2**20),
        name="prepare",
    )(partners, keys, values)


def loss_weight(all_tokens, padding_refs, width):
    last = padding_refs[0].shape[1] - 1
    padded = sum([ref[0, last] for ref in padding_refs])
    return F32(all_tokens) / jnp.full((1, width), all_tokens - padded, jnp.int32).astype(F32)


def finish_kernel(all_tokens, counts, *refs):
    padding_refs, (gq_ref, own_ref, *rest) = refs[:counts], refs[counts:]
    *parts, scaled_ref, gk_ref, gv_ref = rest
    weight = loss_weight(all_tokens, padding_refs, gq_ref.shape[2])
    scaled_ref[0] = (gq_ref[0].astype(F32) * weight).astype(BF16)
    for which, out_ref in enumerate((gk_ref, gv_ref)):
        value = own_ref[which]
        for part in parts:
            value = value + part[which].astype(F32)
        out_ref[0] = (value * weight[:, : value.shape[1]]).astype(BF16)


def finish(all_tokens, paddings, grad_q, own, parts):
    steps = 4
    rows = grad_q.shape[1]
    smem = pl.BlockSpec(memory_space=pltpu.SMEM)
    wide = pl.BlockSpec((1, rows, grad_q.shape[2] // steps), lambda j: (0, 0, j))
    pair = pl.BlockSpec((2, rows, own.shape[2] // steps), lambda j: (0, 0, j))
    one = pl.BlockSpec((1, rows, own.shape[2] // steps), lambda j: (0, 0, j))
    keys = jax.ShapeDtypeStruct((1,) + own.shape[1:], BF16)
    return pl.pallas_call(
        functools.partial(finish_kernel, all_tokens, len(paddings)),
        grid=(steps,),
        in_specs=[smem] * len(paddings) + [wide, pair] + [pair] * len(parts),
        out_specs=[wide, one, one],
        out_shape=[jax.ShapeDtypeStruct(grad_q.shape, BF16), keys, keys],
        compiler_params=pltpu.CompilerParams(vmem_limit_bytes=60 * 2**20),
        name="finish",
    )(*paddings, grad_q, own, *parts)


def fetch(bits, step, both, lengths):
    received = [swapped(both, "ctx", 1 << bit) for bit in bits]
    return received, lengths + swapped(lengths, "dp", step)


def give_back(bits, steps, back, padding):
    returned = [swapped(part, "ctx", 1 << bit) for bit, part in list(zip(bits, back))[::-1]]
    return returned, [swapped(padding, "dp", step) for step in steps]


def on_device(queries, keys, values, grad_out, doc_lengths, block_of_slot, partners):
    rounds = partners.shape[0]
    seqs, ranks = lax.axis_size("dp"), lax.axis_size("ctx")
    choices = list(itertools.combinations(range(ranks.bit_length() - 1), rounds))
    steps = [1 << step for step in reversed(range(seqs.bit_length() - 1))]
    rank = lax.axis_index("ctx").astype(jnp.int32).reshape(1)
    both, which = prepare(choices, partners, keys, values)
    fetches = [functools.partial(fetch, bits, steps[0]) for bits in choices]
    received, padding = lax.switch(which[0], fetches, both, doc_lengths)
    other = swapped(padding, "dp", steps[1])
    attended, grad_q, own, *back = attention(
        rank, which, doc_lengths, block_of_slot, queries, grad_out, keys, values, received
    )
    other, back = lax.optimization_barrier((other, back))
    gives = [functools.partial(give_back, bits, (1, 2, 3)) for bits in choices]
    padding = padding + other
    returned, others = lax.switch(which[0], gives, back, padding)
    all_tokens = seqs * ranks * queries.shape[1]
    grad_q, grad_k, grad_v = finish(all_tokens, [padding] + others, grad_q, own, returned)
    return attended, grad_q, grad_k, grad_v


def solution(mesh):
    rows = P("dp", "ctx", None)
    in_specs = (rows, rows, rows, rows, P("dp", None), P(), P())
    return jax.shard_map(
        on_device, mesh=mesh, in_specs=in_specs, out_specs=(rows,) * 4, check_vma=False
    )
```
